256 devices in a mesh: dp: 64 (over z_lo, y, x), tensor: 4 (over z_hi, core).
Axes of the slice: x: 4, y: 4, z: 8 (z_hi: 2, z_lo: 4; z = z_hi * 4 + z_lo), core: 2. Of those that a mesh axis runs over, the one named last changes fastest.
Arguments:
- teacher_partial: bfloat16 [4, 16384, 8192], P('tensor', 'dp'), may hold values from -6 to 6
- teacher_resid: bfloat16 [16384, 8192], P('dp'), may hold values from -400 to 400
- norm_gain: float32 [8192], P('tensor'), may hold values from 0.1 to 1.9
- projector: bfloat16 [2048, 8192], P('dp', 'tensor'), may hold values from -0.0625 to 0.0625
- student_hidden: bfloat16 [16384, 2048], P('dp'), may hold values from -6 to 6
Outputs:
- distill_error: bfloat16 [16384, 2048], P(('dp', 'tensor'))
- projector_grad: float32 [2048, 8192], P('dp', 'tensor')
The draws below stay inside these ranges and needn't reach their ends.
All inputs are finite; a program needn't handle non-finite values.
Results may differ from the reference program's by a relative error of at most 0.015.
Values may be sent and summed in bfloat16 or wider, within the bound.
A program may use at most 128 MiB of HBM per device.

```python
import jax
import jax.numpy as jnp
from jax import lax

DT = 8192
PW = 2048
TOK_DEV = 256
TOKENS = 16384
N_TENSOR = 4


def draw_teacher_resid(key, part):
    key = jax.random.fold_in(key, 11)
    key_base, key_rows = jax.random.split(key, 2)
    column_pos = jnp.arange(DT, dtype=jnp.float32) / DT
    values = jax.random.normal(key_base, (TOKENS, DT), jnp.float32)
    row_scale = 10.0 ** jax.random.uniform(key_rows, (TOKENS, 1), jnp.float32)
    return (0.25 * values * row_scale * 10.0 ** column_pos[None, :]).astype(jnp.bfloat16)


def level_of(rng, dims, cuts, smallest, top_value):
    factor_of = 1.0
    for axis_at, shards_of in cuts:
        draws = jax.random.uniform(jax.random.fold_in(jax.random.fold_in(rng, 6), axis_at), (shards_of,), jnp.float32, smallest / len(cuts), top_value / len(cuts))
        factor_of = factor_of * jnp.repeat(jnp.exp(draws), dims[axis_at] // shards_of).reshape((-1,) + (1,) * (len(dims) - 1 - axis_at))
    return factor_of


def noise(own_key, extent, deviation, reach, cuts=(), kind=jnp.bfloat16):
    loudness = level_of(own_key, extent, cuts, -0.22, 0.18) if cuts else 1.0
    array = jax.random.normal(own_key, extent, jnp.float32) * deviation * loudness
    return jnp.minimum(jnp.maximum(array, -reach), reach).astype(kind)


def setup_inputs(seed: int = 0) -> dict:
    streams_of = jax.random.split(jax.random.key(seed), 6)
    return {
        "teacher_partial": noise(streams_of[0], (N_TENSOR, TOKENS, DT), 1.0, 6.0, ((0, 4), (1, 64))),
        "teacher_resid": draw_teacher_resid(jax.random.fold_in(streams_of[5], 71), 0),
        "norm_gain": jnp.clip(1.0 + 0.18 * jax.random.normal(streams_of[2], (DT,), jnp.float32), 0.1, 1.9),
        "projector": noise(streams_of[3], (PW, DT), DT ** -0.5, 0.0625, ((0, 64), (1, 4))),
        "student_hidden": noise(streams_of[4], (TOKENS, PW), 1.0, 6.0, ((0, 64),)),
    }


def reference(teacher_partial, teacher_resid, norm_gain, projector, student_hidden):
    hidden = teacher_resid.astype(jnp.float32)
    for member in range(N_TENSOR):
        hidden = hidden + teacher_partial[member].astype(jnp.float32)
    mean_sq = lax.optimization_barrier(jnp.mean(hidden * hidden, axis=1, keepdims=True))
    inv_rms = lax.rsqrt(mean_sq + 1e-05)
    normed = (hidden * inv_rms * norm_gain[None, :]).astype(jnp.bfloat16)
    projected = jnp.dot(normed, projector.T, preferred_element_type=jnp.float32)
    mismatch = (projected - student_hidden.astype(jnp.float32)).astype(jnp.bfloat16)
    gradient = jnp.dot(mismatch.T, normed, preferred_element_type=jnp.float32) * (1.0 / TOK_DEV)
    return (mismatch, gradient)
```

```python
import jax
import jax.numpy as jnp
from jax import lax
from jax.experimental import pallas as pl
from jax.experimental.pallas import tpu as pltpu
from jax.sharding import PartitionSpec as P

MESH_ID = pl.DeviceIdType.MESH
F32 = jnp.float32
BF16 = jnp.bfloat16
EPS = 1e-05
DT = 8192
NX_, NY_, NZL, NZ = 4, 4, 4, 8
K = 4
TILE = 512


def dot_nt(a, b):
    return lax.dot_general(a, b, (((1,), (1,)), ((), ())), preferred_element_type=F32)


def dot_tn(a, b):
    return lax.dot_general(a, b, (((0,), (0,)), ((), ())), preferred_element_type=F32)


def kernel(
    tp, res, gain, proj, stu, out_e, out_g,
    t_own, t_rem, r_own, hid, z_out, z_in, gains, sq_out, sq_in, n_out, norm,
    w, st_raw, st_out, st_in, pp, pp_out, pp_in, q_out, q_in, err, e_in, grad, g_out, g_in, f_out, f_in,
    send_sem, recv_sem, local_sem,
):
    dp = lax.axis_index("dp")
    tensor = lax.axis_index("tensor")
    x = lax.rem(dp, NX_)
    y = lax.rem(dp // NX_, NY_)
    zl = dp // (NX_ * NY_)
    zh = tensor // 2
    c = lax.rem(tensor, 2)
    z = zh * NZL + zl
    other = 1 - c

    def device(dx=0, dy=0, dz=0, dc=0):
        x1 = lax.rem(x + dx, NX_)
        y1 = lax.rem(y + dy, NY_)
        z1 = lax.rem(z + dz, NZ)
        c1 = lax.rem(c + dc, 2)
        return (lax.rem(z1, NZL) * (NX_ * NY_) + y1 * NX_ + x1, (z1 // NZL) * 2 + c1)

    counts = {"remote": 0, "local": 0}
    sends = []

    def remote(src, dst, **offset):
        i = counts["remote"]
        counts["remote"] += 1
        copy = pltpu.make_async_remote_copy(
            src, dst, send_sem.at[i], recv_sem.at[i], device_id=device(**offset), device_id_type=MESH_ID
        )
        copy.start()
        sends.append(copy)
        return copy

    def local(src, dst):
        i = counts["local"]
        counts["local"] += 1
        copy = pltpu.make_async_copy(src, dst, local_sem.at[i])
        copy.start()
        return copy

    def cols(index, width):
        return pl.ds(pl.multiple_of(index * width, width), width)

    early = [
        [local(tp.at[1 - zh, :, k, :, cols(2 * h + c, 2048)], t_own.at[0, :, k, :, pl.ds(h * 2048, 2048)]) for h in range(2)]
        for k in range(K)
    ]
    late = [local(tp.at[zh, :, :, :, cols(2 * h + c, 2048)], t_own.at[1, :, :, :, pl.ds(h * 2048, 2048)]) for h in range(2)]
    late += [local(res.at[zh, :, :, :, cols(2 * h + c, 2048)], r_own.at[:, :, :, pl.ds(h * 2048, 2048)]) for h in range(2)]
    late_gain = local(gain, gains.at[zh])
    late_student = local(stu.at[zh, c], st_raw)
    late_w = local(proj.at[:, cols(x, TILE)], w.at[z, pl.ds(pl.multiple_of(x * 32, 32), 32)])

    partners = [dict(dc=1)]
    partners += [dict(dz=d) for d in range(1, NZ)]
    partners += [dict(dx=d, dc=e) for d in range(1, NX_) for e in range(2)]
    partners += [dict(dy=d) for d in range(1, NY_)]
    barrier = pltpu.get_barrier_semaphore()
    for offset in partners:
        pl.semaphore_signal(barrier, inc=1, device_id=device(**offset), device_id_type=MESH_ID)
    pl.semaphore_wait(barrier, len(partners))

    early_in = [
        [
            remote(tp.at[1 - zh, :, k, :, cols(2 * h + other, 2048)], t_rem.at[0, :, k, :, pl.ds(h * 2048, 2048)], dc=1)
            for h in range(2)
        ]
        for k in range(K)
    ]
    late_in = [
        remote(tp.at[zh, :, :, :, cols(2 * h + other, 2048)], t_rem.at[1, :, :, :, pl.ds(h * 2048, 2048)], dc=1)
        for h in range(2)
    ]
    w_x = [
        remote(proj.at[:, cols(lax.rem(x + d, NX_), TILE)], w.at[z, pl.ds(pl.multiple_of(x * 32, 32), 32)], dx=d)
        for d in range(1, NX_)
    ]

    z_copy = []
    for k in range(K):
        for h in range(2):
            early[k][h].wait()
            early_in[k][h].wait_recv()

        @pl.loop(0, 4096 // TILE)
        def _(t, k=k):
            at = cols(t, TILE)
            pair = t_own[0, :, k, :, at].astype(F32) + t_rem[0, :, k, :, at].astype(F32)
            z_out[k, :, :, at] = pair.astype(BF16)

        z_copy.append(remote(z_out.at[k], z_in.at[k], dz=4))

    late_w.wait()
    for copy in w_x:
        copy.wait_recv()

    def ring_step(s):
        right = lax.rem(z + NZ - (s - 1), NZ)
        left = lax.rem(z + (s - 1), NZ)
        copies = [remote(w.at[right], w.at[right], dz=1)]
        if s < 4:
            copies.append(remote(w.at[left], w.at[left], dz=NZ - 1))
        return copies

    ring = ring_step(1)
    gain_in = remote(gain, gains.at[zh], dz=4)

    for copy in late:
        copy.wait()
    for copy in late_in:
        copy.wait_recv()
    for k in range(K):

        @pl.loop(0, 4096 // TILE)
        def _(t, k=k):
            at = cols(t, TILE)
            hid[k, :, :, at] = (
                r_own[:, k, :, at].astype(F32) + t_own[1, :, k, :, at].astype(F32) + t_rem[1, :, k, :, at].astype(F32)
            )

    late_student.wait()
    for y1 in range(NY_):
        for b in range(NZL):
            st_out[y1, :, :, b * 128 : (b + 1) * 128] = st_raw[:, :, b * 512 + y1 * 128 : b * 512 + (y1 + 1) * 128]
    st_own = local(st_out.at[y], st_in.at[y])
    st_copy = [remote(st_out.at[lax.rem(y + d, NY_)], st_in.at[y], dy=d) for d in range(1, NY_)]

    for copy in ring:
        copy.wait_recv()
    ring = ring_step(2)
    late_gain.wait()
    gain_in.wait_recv()

    x_copy, y_copy, p_copy, q_copy, e_copy, o_copy = {}, {}, {}, {}, {}, {}

    def normalise(k):
        z_copy[k].wait_recv()

        def add(t, total):
            at = cols(t, TILE)
            value = hid[k, :, :, at] + z_in[k, :, :, at].astype(F32)
            hid[k, :, :, at] = value
            square = value * value
            for b in range(TILE // 128):
                total = total + square[:, :, b * 128 : (b + 1) * 128]
            return total

        total = lax.fori_loop(0, 4096 // TILE, add, jnp.zeros((2, 16, 128), F32))
        sq_out[k] = total
        copy = remote(sq_out.at[k], sq_in.at[k], dc=1)
        copy.wait_recv()
        whole = jnp.sum(sq_out[k] + sq_in[k], axis=-1, keepdims=True)
        inv = lax.rsqrt(whole / DT + EPS)
        for h in range(2):

            @pl.loop(0, NX_)
            def _(x1, h=h):
                at = pl.ds(pl.multiple_of(h * 2048 + x1 * TILE, TILE), TILE)
                g = gains[h, :, cols(x1, TILE)]
                n_out[k, x1, :, :, h * TILE : (h + 1) * TILE] = (hid[k, :, :, at] * inv * g[None]).astype(BF16)

        x_copy[k] = [local(n_out.at[k, x], norm.at[k, y, x])]
        x_copy[k] += [remote(n_out.at[k, lax.rem(x + d, NX_)], norm.at[k, y, x], dx=d) for d in range(1, NX_)]

    def gather_y(k):
        x_copy[k][0].wait()
        for copy in x_copy[k][1:]:
            copy.wait_recv()
        y_copy[k] = [remote(norm.at[k, y], norm.at[k, y], dy=d) for d in range(1, NY_)]

    def project(k):
        for copy in y_copy[k]:
            copy.wait_recv()
        for mine in (False, True):
            half = c if mine else other
            for n in range(2):
                total = None
                for h in range(2):
                    rows = norm[k, :, :, half, :, h * TILE : (h + 1) * TILE].reshape(256, TILE)
                    weights = w[4 * h + 2 * n : 4 * h + 2 * n + 2].reshape(256, TILE)
                    part = dot_nt(rows, weights)
                    total = part if total is None else total + part
                total = total.reshape(NY_, NX_, 16, 256)
                if mine:
                    pp[:, :, :, n * 256 : (n + 1) * 256] = total
                else:
                    pp_out[k, :, :, :, n * 256 : (n + 1) * 256] = total.astype(BF16)
            if not mine:
                p_copy[k] = remote(pp_out.at[k], pp_in.at[k], dc=1)

    def pair_up(k):
        p_copy[k].wait_recv()

        @pl.loop(0, NY_)
        def _(y1):
            total = pp[y1] + pp_in[k, y1].astype(F32)
            pp[y1] = total
            q_out[k, y1] = total.astype(BF16)

        q_copy[k] = [remote(q_out.at[k, :, lax.rem(x + d, NX_)], q_in.at[k, x], dx=d) for d in range(1, NX_)]

    def subtract(k):
        for copy in q_copy[k]:
            copy.wait_recv()

        @pl.loop(0, NY_)
        def _(y1):
            total = pp[y1, x]
            for d in range(1, NX_):
                total = total + q_in[k, lax.rem(x + d, NX_), y1].astype(F32)
            err[k, y1, x, c] = (total - st_in[y1, k].astype(F32)).astype(BF16)

        e_copy[k] = [
            remote(err.at[k, :, x, c], err.at[k, :, x, c], dx=d, dc=e)
            for d in range(NX_) for e in range(2) if (d, e) != (0, 0)
        ]
        e_in[y, k] = err[k, y, x, c]
        o_copy[k] = [remote(err.at[k, lax.rem(y + d, NY_), x, c], e_in.at[y, k], dy=d) for d in range(1, NY_)]

    def accumulate(k):
        for copy in e_copy[k]:
            copy.wait_recv()
        e = err[k].reshape(512, 512)
        for h in range(2):
            n = norm[k, :, :, :, :, h * TILE : (h + 1) * TILE].reshape(512, TILE)
            part = dot_tn(e, n).reshape(NZL, 128, TILE)
            grad[h] = part if k == 0 else grad[h] + part

    for copy in st_copy:
        copy.wait_recv()
    st_own.wait()

    for k in range(K + 1):
        if k < K:
            normalise(k)
        if k == 0 or k == 1:
            for copy in ring:
                copy.wait_recv()
            ring = ring_step(3 + k)
        if k == 1:
            for copy in ring:
                copy.wait_recv()
        if k >= 1:
            project(k - 1)
        if k < K:
            gather_y(k)
        if k >= 1:
            pair_up(k - 1)
        if k >= 2:
            accumulate(k - 2)
        if k >= 1:
            subtract(k - 1)
    accumulate(K - 1)

    for h in range(2):
        for b in range(NZL):
            g_out[h * NZL + b] = grad[h, b].astype(BF16)
    g_copy = [remote(g_out.at[lax.rem(z + d, NZ)], g_in.at[z], dz=d) for d in range(1, NZ)]
    for k in range(K):
        for copy in o_copy[k]:
            copy.wait_recv()
    for y1 in range(NY_):
        for b in range(NZL):
            out_e[:, :, b * 512 + y1 * 128 : b * 512 + (y1 + 1) * 128] = e_in[y1, :, :, b * 128 : (b + 1) * 128]
    for copy in g_copy:
        copy.wait_recv()

    @pl.loop(0, NX_)
    def _(x1):
        at = pl.ds(pl.multiple_of(x1 * 32, 32), 32)
        total = grad[zh, zl, at]
        for d in range(1, NZ):
            total = total + g_in[lax.rem(z + d, NZ), at].astype(F32)
        f_out[x1] = total * (1.0 / 256)

    f_in[x] = f_out[x]
    f_copy = [remote(f_out.at[lax.rem(x + d, NX_)], f_in.at[x], dx=d) for d in range(1, NX_)]
    for copy in f_copy:
        copy.wait_recv()
    for x1 in range(NX_):
        out_g[:, x1 * TILE : (x1 + 1) * TILE] = f_in[x1]
    for copy in sends:
        copy.wait_send()


def body(teacher_partial, teacher_resid, norm_gain, projector, student_hidden):
    tp = teacher_partial.reshape(2, 2, K, 16, DT)
    res = teacher_resid.reshape(2, 2, K, 16, DT)
    stu = student_hidden.reshape(2, 2, K, 16, 2048)
    hbm = pl.BlockSpec(memory_space=pl.ANY)
    vmem = pl.BlockSpec(memory_space=pltpu.VMEM)
    error, gradient = pl.pallas_call(
        kernel,
        out_shape=(jax.ShapeDtypeStruct((K, 16, 2048), BF16), jax.ShapeDtypeStruct((32, 2048), F32)),
        in_specs=[hbm] * 5,
        out_specs=(vmem, vmem),
        scratch_shapes=[
            pltpu.VMEM((2, 2, K, 16, 4096), BF16),
            pltpu.VMEM((2, 2, K, 16, 4096), BF16),
            pltpu.VMEM((2, K, 16, 4096), BF16),
            pltpu.VMEM((K, 2, 16, 4096), F32),
            pltpu.VMEM((K, 2, 16, 4096), BF16),
            pltpu.VMEM((K, 2, 16, 4096), BF16),
            pltpu.VMEM((2, 1, 2048), F32),
            pltpu.VMEM((K, 2, 16, 128), F32),
            pltpu.VMEM((K, 2, 16, 128), F32),
            pltpu.VMEM((K, 4, 2, 16, 1024), BF16),
            pltpu.VMEM((K, 4, 4, 2, 16, 1024), BF16),
            pltpu.VMEM((8, 128, 512), BF16),
            pltpu.VMEM((K, 16, 2048), BF16),
            pltpu.VMEM((4, K, 16, 512), BF16),
            pltpu.VMEM((4, K, 16, 512), BF16),
            pltpu.VMEM((4, 4, 16, 512), F32),
            pltpu.VMEM((K, 4, 4, 16, 512), BF16),
            pltpu.VMEM((K, 4, 4, 16, 512), BF16),
            pltpu.VMEM((K, 4, 4, 16, 512), BF16),
            pltpu.VMEM((K, 4, 4, 16, 512), BF16),
            pltpu.VMEM((K, 4, 4, 2, 16, 512), BF16),
            pltpu.VMEM((4, K, 16, 512), BF16),
            pltpu.VMEM((2, 4, 128, 512), F32),
            pltpu.VMEM((8, 128, 512), BF16),
            pltpu.VMEM((8, 128, 512), BF16),
            pltpu.VMEM((4, 32, 512), F32),
            pltpu.VMEM((4, 32, 512), F32),
            pltpu.SemaphoreType.DMA((128,)),
            pltpu.SemaphoreType.DMA((128,)),
            pltpu.SemaphoreType.DMA((32,)),
        ],
        compiler_params=pltpu.CompilerParams(
            collective_id=0, has_side_effects=True, vmem_limit_bytes=56 << 20
        ),
        name="distill",
    )(tp, res, norm_gain.reshape(1, -1), projector, stu)
    return error.reshape(-1, 2048), gradient


def solution(mesh):
    placed = (P("tensor", "dp", None), P("dp", None), P("tensor"), P("dp", "tensor"), P("dp", None))
    return jax.shard_map(
        body,
        mesh=mesh,
        in_specs=placed,
        out_specs=(P(("dp", "tensor"), None), P("dp", "tensor")),
        check_vma=False,
    )
```

```python
import jax
import jax.numpy as jnp
from jax import lax
from jax.experimental import pallas as pl
from jax.experimental.pallas import tpu as pltpu
from jax.sharding import PartitionSpec as P

MESH_ID = pl.DeviceIdType.MESH
F32 = jnp.float32
BF16 = jnp.bfloat16
EPS = 1e-05
DT = 8192
NX_, NY_, NZL, NZ = 4, 4, 4, 8
K = 4
TILE = 512


def dot_nt(a, b):
    return lax.dot_general(a, b, (((1,), (1,)), ((), ())), preferred_element_type=F32)


def dot_tn(a, b):
    return lax.dot_general(a, b, (((0,), (0,)), ((), ())), preferred_element_type=F32)


def kernel(
    tp, res, gain, proj, stu, out_e, out_g,
    t_own, t_rem, r_own, hid, z_out, z_in, gains, sq_out, sq_in, n_out, norm,
    w, st_raw, st_out, st_in, pp, pp_out, pp_in, q_out, q_in, err, e_in, grad, g_out, g_in, f_out, f_in,
    send_sem, recv_sem, local_sem, ready,
):
    dp = lax.axis_index("dp")
    tensor = lax.axis_index("tensor")
    x = lax.rem(dp, NX_)
    y = lax.rem(dp // NX_, NY_)
    zl = dp // (NX_ * NY_)
    zh = tensor // 2
    c = lax.rem(tensor, 2)
    z = zh * NZL + zl
    other = 1 - c

    def device(dx=0, dy=0, dz=0, dc=0):
        x1 = lax.rem(x + dx, NX_)
        y1 = lax.rem(y + dy, NY_)
        z1 = lax.rem(z + dz, NZ)
        c1 = lax.rem(c + dc, 2)
        return (lax.rem(z1, NZL) * (NX_ * NY_) + y1 * NX_ + x1, (z1 // NZL) * 2 + c1)

    counts = {"remote": 0, "local": 0}
    sends = []

    def remote(src, dst, **offset):
        i = counts["remote"]
        counts["remote"] += 1
        copy = pltpu.make_async_remote_copy(
            src, dst, send_sem.at[i], recv_sem.at[i], device_id=device(**offset), device_id_type=MESH_ID
        )
        copy.start()
        sends.append(copy)
        return copy

    def local(src, dst):
        i = counts["local"]
        counts["local"] += 1
        copy = pltpu.make_async_copy(src, dst, local_sem.at[i])
        copy.start()
        return copy

    def cols(index, width):
        return pl.ds(pl.multiple_of(index * width, width), width)

    early = [
        [local(tp.at[1 - zh, :, k, :, cols(2 * h + c, 2048)], t_own.at[0, :, k, :, pl.ds(h * 2048, 2048)]) for h in range(2)]
        for k in range(K)
    ]
    late = [local(tp.at[zh, :, :, :, cols(2 * h + c, 2048)], t_own.at[1, :, :, :, pl.ds(h * 2048, 2048)]) for h in range(2)]
    late += [local(res.at[zh, :, :, :, cols(2 * h + c, 2048)], r_own.at[:, :, :, pl.ds(h * 2048, 2048)]) for h in range(2)]
    late_gain = local(gain, gains.at[zh])
    late_student = local(stu.at[zh, c], st_raw)
    late_w = local(proj.at[:, cols(x, TILE)], w.at[z, pl.ds(pl.multiple_of(x * 32, 32), 32)])

    partners = [dict(dc=1)]
    partners += [dict(dz=d) for d in range(1, NZ)]
    partners += [dict(dx=d) for d in range(1, NX_)]
    partners += [dict(dy=d) for d in range(1, NY_)]
    barrier = pltpu.get_barrier_semaphore()
    for offset in partners:
        pl.semaphore_signal(barrier, inc=1, device_id=device(**offset), device_id_type=MESH_ID)
    pl.semaphore_wait(barrier, len(partners))

    gain_in = remote(gain, gains.at[zh], dz=4)
    early_in = [
        [
            remote(tp.at[1 - zh, :, k, :, cols(2 * h + other, 2048)], t_rem.at[0, :, k, :, pl.ds(h * 2048, 2048)], dc=1)
            for h in range(2)
        ]
        for k in range(K)
    ]
    late_in = [
        remote(tp.at[zh, :, :, :, cols(2 * h + other, 2048)], t_rem.at[1, :, :, :, pl.ds(h * 2048, 2048)], dc=1)
        for h in range(2)
    ]
    w_x = [
        remote(proj.at[:, cols(lax.rem(x + d, NX_), TILE)], w.at[z, pl.ds(pl.multiple_of(x * 32, 32), 32)], dx=d)
        for d in range(1, NX_)
    ]

    pieces = [(k, half, h) for k in range(K) for half in range(2) for h in range(2)]
    z_copy = {}

    def send_pieces(first, last):
        for k, half, h in pieces[first:last]:
            at = pl.ds(h * 2048, 2048)
            z_copy[k, half, h] = remote(z_out.at[k, half, :, at], z_in.at[k, half, :, at], dz=4)

    def ring_step(s):
        right = lax.rem(z + NZ - (s - 1), NZ)
        left = lax.rem(z + (s - 1), NZ)
        return [remote(w.at[right], w.at[right], dz=1), remote(w.at[left], w.at[left], dz=NZ - 1)]

    def arrived(copies):
        for copy in copies:
            copy.wait_recv()

    def pair_sum(k):
        for h in range(2):
            early[k][h].wait()
            early_in[k][h].wait_recv()

        @pl.loop(0, 4096 // TILE)
        def _(t):
            at = cols(t, TILE)
            pair = t_own[0, :, k, :, at].astype(F32) + t_rem[0, :, k, :, at].astype(F32)
            z_out[k, :, :, at] = pair.astype(BF16)

    pair_sum(0)
    send_pieces(0, 2)
    for k in range(1, K):
        pair_sum(k)
    late_w.wait()
    arrived(w_x)
    ring = ring_step(1)
    far = remote(w.at[z], w.at[z], dz=4)

    for copy in late:
        copy.wait()
    arrived(late_in)
    for k in range(K):

        @pl.loop(0, 4096 // TILE)
        def _(t, k=k):
            at = cols(t, TILE)
            hid[k, :, :, at] = (
                r_own[:, k, :, at].astype(F32) + t_own[1, :, k, :, at].astype(F32) + t_rem[1, :, k, :, at].astype(F32)
            )

    late_student.wait()
    for y1 in range(NY_):
        for b in range(NZL):
            st_out[y1, :, :, b * 128 : (b + 1) * 128] = st_raw[:, :, b * 512 + y1 * 128 : b * 512 + (y1 + 1) * 128]
    st_own = local(st_out.at[y], st_in.at[y])
    st_copy = [remote(st_out.at[lax.rem(y + d, NY_)], st_in.at[y], dy=d) for d in range(1, NY_)]

    arrived(ring)
    ring = ring_step(2)
    send_pieces(2, 3)
    late_gain.wait()
    gain_in.wait_recv()

    x_copy, y_copy, p_copy, q_copy, e_copy, s_copy, o_copy = {}, {}, {}, {}, {}, {}, {}

    def normalise(k):
        arrived([z_copy[k, half, h] for half in range(2) for h in range(2)])

        def add(t, total):
            at = cols(t, TILE)
            value = hid[k, :, :, at] + z_in[k, :, :, at].astype(F32)
            hid[k, :, :, at] = value
            square = value * value
            for b in range(TILE // 128):
                total = total + square[:, :, b * 128 : (b + 1) * 128]
            return total

        total = lax.fori_loop(0, 4096 // TILE, add, jnp.zeros((2, 16, 128), F32))
        sq_out[k] = total
        copy = remote(sq_out.at[k], sq_in.at[k], dc=1)
        copy.wait_recv()
        whole = jnp.sum(sq_out[k] + sq_in[k], axis=-1, keepdims=True)
        inv = lax.rsqrt(whole / DT + EPS)
        for h in range(2):

            @pl.loop(0, NX_)
            def _(x1, h=h):
                at = pl.ds(pl.multiple_of(h * 2048 + x1 * TILE, TILE), TILE)
                g = gains[h, :, cols(x1, TILE)]
                n_out[k, x1, :, :, h * TILE : (h + 1) * TILE] = (hid[k, :, :, at] * inv * g[None]).astype(BF16)

        x_copy[k] = [local(n_out.at[k, x], norm.at[k, y, x])]
        x_copy[k] += [remote(n_out.at[k, lax.rem(x + d, NX_)], norm.at[k, y, x], dx=d) for d in range(1, NX_)]

    def gather_y(k):
        x_copy[k][0].wait()
        for copy in x_copy[k][1:]:
            copy.wait_recv()
        y_copy[k] = [remote(norm.at[k, y], norm.at[k, y], dy=d) for d in (1, NY_ - 1)]

    def forward_y(k):
        for i, d in enumerate((1, NY_ - 1)):
            y_copy[k][i].wait_recv()
            rows = norm.at[k, lax.rem(y + NY_ - d, NY_), 2 * i : 2 * i + 2]
            y_copy[k].append(remote(rows, rows, dy=d))

    def project(k):
        for copy in y_copy[k][2:]:
            copy.wait_recv()
        for mine in (False, True):
            half = c if mine else other
            for n in range(2):
                total = None
                for h in range(2):
                    rows = norm[k, :, :, half, :, h * TILE : (h + 1) * TILE].reshape(256, TILE)
                    weights = w[4 * h + 2 * n : 4 * h + 2 * n + 2].reshape(256, TILE)
                    part = dot_nt(rows, weights)
                    total = part if total is None else total + part
                total = total.reshape(NY_, NX_, 16, 256)
                if mine:
                    pp[:, :, :, n * 256 : (n + 1) * 256] = total
                else:
                    pp_out[k, :, :, :, n * 256 : (n + 1) * 256] = total.astype(BF16)
            if not mine:
                p_copy[k] = remote(pp_out.at[k], pp_in.at[k], dc=1)

    def pair_up(k):
        p_copy[k].wait_recv()

        @pl.loop(0, NY_)
        def _(y1):
            total = pp[y1] + pp_in[k, y1].astype(F32)
            pp[y1] = total
            q_out[k, y1] = total.astype(BF16)

        q_copy[k] = [remote(q_out.at[k, :, lax.rem(x + d, NX_)], q_in.at[k, x], dx=d) for d in range(1, NX_)]

    def subtract(k):
        for copy in q_copy[k]:
            copy.wait_recv()

        @pl.loop(0, NY_)
        def _(y1):
            total = pp[y1, x]
            for d in range(1, NX_):
                total = total + q_in[k, lax.rem(x + d, NX_), y1].astype(F32)
            err[k, y1, x, c] = (total - st_in[y1, k].astype(F32)).astype(BF16)

        e_copy[k] = [remote(err.at[k, :, x, c], err.at[k, :, x, c], dx=d) for d in range(1, NX_)]
        e_in[y, k] = err[k, y, x, c]
        o_copy[k] = [remote(err.at[k, lax.rem(y + d, NY_), x, c], e_in.at[y, k], dy=d) for d in range(1, NY_)]

    def share(k):
        for copy in e_copy[k]:
            copy.wait_recv()
        s_copy[k] = remote(err.at[k, :, :, c], err.at[k, :, :, c], dc=1)

    def accumulate(k):
        s_copy[k].wait_recv()
        e = err[k].reshape(512, 512)
        for h in range(2):
            n = norm[k, :, :, :, :, h * TILE : (h + 1) * TILE].reshape(512, TILE)
            part = dot_tn(e, n).reshape(NZL, 128, TILE)
            grad[h] = part if k == 0 else grad[h] + part

    arrived(st_copy)
    st_own.wait()

    arrived(ring)
    ring = ring_step(3)
    send_pieces(3, 4)
    arrived(ring)
    arrived([far])
    send_pieces(4, 6)
    pl.semaphore_signal(ready.at[0], inc=1, device_id=device(dc=1), device_id_type=MESH_ID)
    pl.semaphore_wait(ready.at[0], 1)
    for d in range(1, NZ):
        pl.semaphore_signal(ready.at[1], inc=1, device_id=device(dz=d), device_id_type=MESH_ID)
    pl.semaphore_wait(ready.at[1], NZ - 1)
    send_pieces(6, len(pieces))
    normalise(0)
    gather_y(0)
    forward_y(0)
    for k in range(1, K + 1):
        if k < K:
            normalise(k)
        if k >= 2:
            subtract(k - 2)
        if k < K:
            gather_y(k)
        project(k - 1)
        if k >= 2:
            share(k - 2)
        pair_up(k - 1)
        if 2 <= k < K:
            accumulate(k - 2)
        if k < K:
            forward_y(k)
    for k in range(K - 1, K + 1):
        if k == K:
            subtract(K - 1)
            share(K - 1)
        accumulate(k - 1)

    def hops(sub, way):
        return 4 if sub == way else 3

    g_copy = {}
    for s in range(1, 5):
        for sub in range(2):
            for way in range(2):
                n = hops(sub, way)
                if s > n:
                    continue
                far = n + 1 - s
                d = lax.rem(z + (far if way == 0 else NZ - far), NZ)
                total = grad[d // NZL, lax.rem(d, NZL), sub * 64 : (sub + 1) * 64]
                if s > 1:
                    g_copy[sub, way, s - 1].wait_recv()
                    total = total + g_in[sub, way, s - 2].astype(F32)
                g_out[sub, way, s - 1] = total.astype(BF16)
                g_copy[sub, way, s] = remote(
                    g_out.at[sub, way, s - 1], g_in.at[sub, way, s - 1], dz=1 if way == 0 else NZ - 1
                )
        if s == 1:
            for k in range(K):
                arrived(o_copy[k])
            for y1 in range(NY_):
                for b in range(NZL):
                    out_e[:, :, b * 512 + y1 * 128 : b * 512 + (y1 + 1) * 128] = e_in[y1, :, :, b * 128 : (b + 1) * 128]
    for x1 in range(NX_):
        sub, part = divmod(x1, 2)
        total = grad[zh, zl, x1 * 32 : (x1 + 1) * 32]
        for way in range(2):
            n = hops(sub, way)
            if part == 0:
                g_copy[sub, way, n].wait_recv()
            total = total + g_in[sub, way, n - 1, part * 32 : (part + 1) * 32].astype(F32)
        f_out[x1] = total * (1.0 / 256)

    f_in[x] = f_out[x]
    f_copy = [remote(f_out.at[lax.rem(x + d, NX_)], f_in.at[x], dx=d) for d in range(1, NX_)]
    for copy in f_copy:
        copy.wait_recv()
    for x1 in range(NX_):
        out_g[:, x1 * TILE : (x1 + 1) * TILE] = f_in[x1]
    for copy in sends:
        copy.wait_send()


def place(error, gradient, out_e, out_g):
    out_e[...] = error[...]
    out_g[...] = gradient[...]


def body(teacher_partial, teacher_resid, norm_gain, projector, student_hidden):
    tp = teacher_partial.reshape(2, 2, K, 16, DT)
    res = teacher_resid.reshape(2, 2, K, 16, DT)
    stu = student_hidden.reshape(2, 2, K, 16, 2048)
    hbm = pl.BlockSpec(memory_space=pl.ANY)
    vmem = pl.BlockSpec(memory_space=pltpu.VMEM)
    error, gradient = pl.pallas_call(
        kernel,
        out_shape=(jax.ShapeDtypeStruct((K, 16, 2048), BF16), jax.ShapeDtypeStruct((32, 2048), F32)),
        in_specs=[hbm] * 5,
        out_specs=(vmem, vmem),
        scratch_shapes=[
            pltpu.VMEM((2, 2, K, 16, 4096), BF16),
            pltpu.VMEM((2, 2, K, 16, 4096), BF16),
            pltpu.VMEM((2, K, 16, 4096), BF16),
            pltpu.VMEM((K, 2, 16, 4096), F32),
            pltpu.VMEM((K, 2, 16, 4096), BF16),
            pltpu.VMEM((K, 2, 16, 4096), BF16),
            pltpu.VMEM((2, 1, 2048), F32),
            pltpu.VMEM((K, 2, 16, 128), F32),
            pltpu.VMEM((K, 2, 16, 128), F32),
            pltpu.VMEM((K, 4, 2, 16, 1024), BF16),
            pltpu.VMEM((K, 4, 4, 2, 16, 1024), BF16),
            pltpu.VMEM((8, 128, 512), BF16),
            pltpu.VMEM((K, 16, 2048), BF16),
            pltpu.VMEM((4, K, 16, 512), BF16),
            pltpu.VMEM((4, K, 16, 512), BF16),
            pltpu.VMEM((4, 4, 16, 512), F32),
            pltpu.VMEM((K, 4, 4, 16, 512), BF16),
            pltpu.VMEM((K, 4, 4, 16, 512), BF16),
            pltpu.VMEM((K, 4, 4, 16, 512), BF16),
            pltpu.VMEM((K, 4, 4, 16, 512), BF16),
            pltpu.VMEM((K, 4, 4, 2, 16, 512), BF16),
            pltpu.VMEM((4, K, 16, 512), BF16),
            pltpu.VMEM((2, 4, 128, 512), F32),
            pltpu.VMEM((2, 2, 4, 64, 512), BF16),
            pltpu.VMEM((2, 2, 4, 64, 512), BF16),
            pltpu.VMEM((4, 32, 512), F32),
            pltpu.VMEM((4, 32, 512), F32),
            pltpu.SemaphoreType.DMA((160,)),
            pltpu.SemaphoreType.DMA((160,)),
            pltpu.SemaphoreType.DMA((32,)),
            pltpu.SemaphoreType.REGULAR((2,)),
        ],
        compiler_params=pltpu.CompilerParams(
            collective_id=0, has_side_effects=True, vmem_limit_bytes=56 << 20
        ),
        name="distill",
    )(tp, res, norm_gain.reshape(1, -1), projector, stu)
    return pl.pallas_call(
        place,
        out_shape=(jax.ShapeDtypeStruct((64, 2048), BF16), jax.ShapeDtypeStruct((32, 2048), F32)),
        in_specs=[vmem] * 2,
        out_specs=(vmem, vmem),
        name="place",
    )(error.reshape(64, 2048), gradient)


def solution(mesh):
    placed = (P("tensor", "dp", None), P("dp", None), P("tensor"), P("dp", "tensor"), P("dp", None))
    return jax.shard_map(
        body,
        mesh=mesh,
        in_specs=placed,
        out_specs=(P(("dp", "tensor"), None), P("dp", "tensor")),
        check_vma=False,
    )
```

```python
import jax
import jax.numpy as jnp
from jax import lax
from jax.experimental import pallas as pl
from jax.experimental.pallas import tpu as pltpu
from jax.sharding import PartitionSpec as P

MESH_ID = pl.DeviceIdType.MESH
F32 = jnp.float32
BF16 = jnp.bfloat16
EPS = 1e-05
DT = 8192
NX_, NY_, NZL, NZ = 4, 4, 4, 8
K = 4
TILE = 512


def dot_nt(a, b):
    return lax.dot_general(a, b, (((1,), (1,)), ((), ())), preferred_element_type=F32)


def dot_tn(a, b):
    return lax.dot_general(a, b, (((0,), (0,)), ((), ())), preferred_element_type=F32)


def kernel(
    tp, res, gain, proj, stu, out_e, out_g,
    t_own, t_rem, r_own, hid, z_out, z_in, gains, sq_out, sq_in, n_out, norm,
    w, st_raw, st_out, st_in, pp, pp_out, pp_in, q_out, q_in, err, e_in, grad, g_out, g_in, f_out, f_in, f_own,
    e_all, g_all,
    send_sem, recv_sem, local_sem, ready,
):
    dp = lax.axis_index("dp")
    tensor = lax.axis_index("tensor")
    x = lax.rem(dp, NX_)
    y = lax.rem(dp // NX_, NY_)
    zl = dp // (NX_ * NY_)
    zh = tensor // 2
    c = lax.rem(tensor, 2)
    z = zh * NZL + zl
    other = 1 - c

    def device(dx=0, dy=0, dz=0, dc=0):
        x1 = lax.rem(x + dx, NX_)
        y1 = lax.rem(y + dy, NY_)
        z1 = lax.rem(z + dz, NZ)
        c1 = lax.rem(c + dc, 2)
        return (lax.rem(z1, NZL) * (NX_ * NY_) + y1 * NX_ + x1, (z1 // NZL) * 2 + c1)

    counts = {"recv": 0, "local": 0}
    sends = {}

    def remote(kind, whole, *pairs, start=True):
        i = counts["recv"]
        counts["recv"] += 1
        j = sends.setdefault(kind, len(sends))
        copies = [
            pltpu.make_async_remote_copy(
                src, dst, send_sem.at[j], recv_sem.at[i], device_id=device(**offset), device_id_type=MESH_ID
            )
            for src, dst, offset in pairs
        ]
        if start:
            for copy in copies:
                copy.start()
        return pltpu.make_async_copy(whole, whole, recv_sem.at[i]), copies

    def local(whole, *pairs):
        i = counts["local"]
        counts["local"] += 1
        for src, dst in pairs:
            pltpu.make_async_copy(src, dst, local_sem.at[i]).start()
        return pltpu.make_async_copy(whole, whole, local_sem.at[i])

    def arrived(group):
        group[0].wait()

    def cols(index, width):
        return pl.ds(pl.multiple_of(index * width, width), width)

    half = [pl.ds(h * 2048, 2048) for h in range(2)]
    mine = [cols(2 * h + c, 2048) for h in range(2)]
    theirs = [cols(2 * h + other, 2048) for h in range(2)]
    early = [
        local(t_own.at[0, :, k], *[(tp.at[1 - zh, :, k, :, mine[h]], t_own.at[0, :, k, :, half[h]]) for h in range(2)])
        for k in range(K)
    ]
    late = [local(t_own.at[1], *[(tp.at[zh, :, :, :, mine[h]], t_own.at[1, :, :, :, half[h]]) for h in range(2)])]
    late += [local(r_own, *[(res.at[zh, :, :, :, mine[h]], r_own.at[:, :, :, half[h]]) for h in range(2)])]
    late_gain = local(gains.at[0], (gain, gains.at[zh]))
    late_student = local(st_raw, (stu.at[zh, c], st_raw))
    own_rows = w.at[z, pl.ds(pl.multiple_of(x * 32, 32), 32)]
    late_w = local(own_rows, (proj.at[:, cols(x, TILE)], own_rows))

    partners = [dict(dc=1)]
    partners += [dict(dz=d) for d in range(1, NZ)]
    partners += [dict(dx=d) for d in range(1, NX_)]
    partners += [dict(dy=d) for d in range(1, NY_)]
    barrier = pltpu.get_barrier_semaphore()
    for offset in partners:
        pl.semaphore_signal(barrier, inc=1, device_id=device(**offset), device_id_type=MESH_ID)
    pl.semaphore_wait(barrier, len(partners))

    gain_in = remote("gain", gains.at[0], (gain, gains.at[zh], dict(dz=4)))
    early_in = [
        remote(
            "early", t_rem.at[0, :, k],
            *[(tp.at[1 - zh, :, k, :, theirs[h]], t_rem.at[0, :, k, :, half[h]], dict(dc=1)) for h in range(2)],
        )
        for k in range(K)
    ]
    late_in = remote(
        "late", t_rem.at[1],
        *[(tp.at[zh, :, :, :, theirs[h]], t_rem.at[1, :, :, :, half[h]], dict(dc=1)) for h in range(2)],
    )
    w_x = remote(
        "w_x", w.at[0, 0:96],
        *[(proj.at[:, cols(lax.rem(x + d, NX_), TILE)], own_rows, dict(dx=d)) for d in range(1, NX_)],
    )

    pieces = [(k, part, h) for k in range(K) for part in range(2) for h in range(2)]
    z_copy = [
        remote(
            "z", z_in.at[k],
            *[
                (z_out.at[k, part, :, half[h]], z_in.at[k, part, :, half[h]], dict(dz=4))
                for part in range(2) for h in range(2)
            ],
            start=False,
        )
        for k in range(K)
    ]

    def send_pieces(first, last):
        for k, part, h in pieces[first:last]:
            z_copy[k][1][2 * part + h].start()

    def ring_step(s):
        right = lax.rem(z + NZ - (s - 1), NZ)
        left = lax.rem(z + (s - 1), NZ)
        return remote(
            "ring", w.at[0:2],
            (w.at[right], w.at[right], dict(dz=1)), (w.at[left], w.at[left], dict(dz=NZ - 1)),
        )

    def pair_sum(k):
        early[k].wait()
        arrived(early_in[k])

        @pl.loop(0, 4096 // TILE)
        def _(t):
            at = cols(t, TILE)
            pair = t_own[0, :, k, :, at].astype(F32) + t_rem[0, :, k, :, at].astype(F32)
            z_out[k, :, :, at] = pair.astype(BF16)

    pair_sum(0)
    send_pieces(0, 2)
    for k in range(1, K):
        pair_sum(k)
    late_w.wait()
    arrived(w_x)
    ring = ring_step(1)
    far = remote("far", w.at[z], (w.at[z], w.at[z], dict(dz=4)))

    for copy in late:
        copy.wait()
    arrived(late_in)
    for k in range(K):

        @pl.loop(0, 4096 // TILE)
        def _(t, k=k):
            at = cols(t, TILE)
            hid[k, :, :, at] = (
                r_own[:, k, :, at].astype(F32) + t_own[1, :, k, :, at].astype(F32) + t_rem[1, :, k, :, at].astype(F32)
            )

    late_student.wait()
    for y1 in range(NY_):
        for b in range(NZL):
            st_out[y1, :, :, b * 128 : (b + 1) * 128] = st_raw[:, :, b * 512 + y1 * 128 : b * 512 + (y1 + 1) * 128]
    st_own = local(st_in.at[y], (st_out.at[y], st_in.at[y]))
    st_copy = remote(
        "student", st_in.at[0:3], *[(st_out.at[lax.rem(y + d, NY_)], st_in.at[y], dict(dy=d)) for d in range(1, NY_)]
    )

    arrived(ring)
    ring = ring_step(2)
    send_pieces(2, 3)
    late_gain.wait()
    arrived(gain_in)

    x_own, x_copy, y_copy, p_copy, q_copy, e_copy, s_copy = {}, {}, {}, {}, {}, {}, {}

    def normalise(k):
        arrived(z_copy[k])

        def add(t, total):
            at = cols(t, TILE)
            value = hid[k, :, :, at] + z_in[k, :, :, at].astype(F32)
            hid[k, :, :, at] = value
            square = value * value
            for b in range(TILE // 128):
                total = total + square[:, :, b * 128 : (b + 1) * 128]
            return total

        sq_out[k] = lax.fori_loop(0, 4096 // TILE, add, jnp.zeros((2, 16, 128), F32))
        arrived(remote("square", sq_in.at[k], (sq_out.at[k], sq_in.at[k], dict(dc=1))))
        whole = jnp.sum(sq_out[k] + sq_in[k], axis=-1, keepdims=True)
        inv = lax.rsqrt(whole / DT + EPS)
        for h in range(2):

            @pl.loop(0, NX_)
            def _(x1, h=h):
                at = pl.ds(pl.multiple_of(h * 2048 + x1 * TILE, TILE), TILE)
                g = gains[h, :, cols(x1, TILE)]
                n_out[k, x1, :, :, h * TILE : (h + 1) * TILE] = (hid[k, :, :, at] * inv * g[None]).astype(BF16)

        own = norm.at[k, y, x]
        x_own[k] = local(own, (n_out.at[k, x], own))
        x_copy[k] = remote(
            "x", n_out.at[k, 0:3], *[(n_out.at[k, lax.rem(x + d, NX_)], own, dict(dx=d)) for d in range(1, NX_)]
        )

    def gather_y(k):
        x_own[k].wait()
        arrived(x_copy[k])
        block = norm.at[k, y]
        y_copy[k] = remote("y", norm.at[k, 0:2], *[(block, block, dict(dy=d)) for d in (1, NY_ - 1)])

    def forward_y(k):
        arrived(y_copy[k])
        blocks = [
            (norm.at[k, lax.rem(y + NY_ - d, NY_), 2 * i : 2 * i + 2], dict(dy=d)) for i, d in enumerate((1, NY_ - 1))
        ]
        y_copy[k] = remote("forward", norm.at[k, 0], *[(block, block, offset) for block, offset in blocks])

    def product(k, half, n):
        total = None
        for h in range(2):
            rows = norm[k, :, :, half, :, h * TILE : (h + 1) * TILE].reshape(256, TILE)
            weights = w[4 * h + 2 * n : 4 * h + 2 * n + 2].reshape(256, TILE)
            part = dot_nt(rows, weights)
            total = part if total is None else total + part
        return total.reshape(NY_, NX_, 16, 256)

    def project(k):
        arrived(y_copy[k])
        for own in (False, True):
            for n in range(2):
                total = product(k, c if own else other, n)
                if own:
                    pp[k % 2, :, :, :, n * 256 : (n + 1) * 256] = total
                else:
                    pp_out[k, :, :, :, n * 256 : (n + 1) * 256] = total.astype(BF16)
            if not own:
                p_copy[k] = remote("pair", pp_in.at[k], (pp_out.at[k], pp_in.at[k], dict(dc=1)))

    def pair_up(k):
        arrived(p_copy[k])

        @pl.loop(0, NY_)
        def _(y1):
            total = pp[k % 2, y1] + pp_in[k, y1].astype(F32)
            pp[k % 2, y1] = total
            q_out[k, y1] = total.astype(BF16)

        q_copy[k] = remote(
            "q", q_in.at[k, 0:3],
            *[(q_out.at[k, :, lax.rem(x + d, NX_)], q_in.at[k, x], dict(dx=d)) for d in range(1, NX_)],
        )

    def subtract(k):
        arrived(q_copy[k])

        @pl.loop(0, NY_)
        def _(y1):
            total = pp[k % 2, y1, x]
            for d in range(1, NX_):
                total = total + q_in[k, lax.rem(x + d, NX_), y1].astype(F32)
            err[k, y1, x, c] = (total - st_in[y1, k].astype(F32)).astype(BF16)

        own = err.at[k, :, x, c]
        e_copy[k] = remote("error", q_in.at[k, 0:3], *[(own, own, dict(dx=d)) for d in range(1, NX_)])
        e_in[y, k] = err[k, y, x, c]
        for i, d in enumerate(range(1, NY_)):
            o_copy[1][3 * k + i].start()

    def share(k):
        arrived(e_copy[k])
        rows = err.at[k, :, :, c]
        s_copy[k] = remote("share", pp_in.at[k], (rows, rows, dict(dc=1)))

    def accumulate(k):
        arrived(s_copy[k])
        e = err[k].reshape(512, 512)
        for h in range(2):
            n = norm[k, :, :, :, :, h * TILE : (h + 1) * TILE].reshape(512, TILE)
            part = dot_tn(e, n).reshape(NZL, 128, TILE)
            grad[h] = part if k == 0 else grad[h] + part

    arrived(st_copy)
    st_own.wait()
    o_copy = remote(
        "out", e_in.at[0:3],
        *[
            (err.at[k, lax.rem(y + d, NY_), x, c], e_in.at[y, k], dict(dy=d))
            for k in range(K) for d in range(1, NY_)
        ],
        start=False,
    )

    arrived(ring)
    ring = ring_step(3)
    send_pieces(3, 4)
    arrived(ring)
    arrived(far)
    send_pieces(4, 6)
    pl.semaphore_signal(ready.at[0], inc=1, device_id=device(dc=1), device_id_type=MESH_ID)
    pl.semaphore_wait(ready.at[0], 1)
    for d in range(1, NZ):
        pl.semaphore_signal(ready.at[1], inc=1, device_id=device(dz=d), device_id_type=MESH_ID)
    normalise(0)
    pl.semaphore_wait(ready.at[1], NZ - 1)
    send_pieces(6, len(pieces))
    gather_y(0)
    for stage, k in (
        (normalise, 1), (forward_y, 0), (gather_y, 1), (project, 0),
        (normalise, 2), (pair_up, 0), (forward_y, 1), (gather_y, 2), (project, 1), (subtract, 0),
        (normalise, 3), (pair_up, 1), (forward_y, 2), (gather_y, 3), (share, 0), (project, 2), (subtract, 1),
        (pair_up, 2), (accumulate, 0), (forward_y, 3), (share, 1), (subtract, 2), (project, 3), (accumulate, 1),
        (pair_up, 3), (share, 2), (subtract, 3), (accumulate, 2), (share, 3), (accumulate, 3),
    ):
        stage(k)

    def hops(sub, way):
        return 4 if sub % 2 == way else 3

    g_copy = {}
    for s in range(1, 5):
        for sub in range(4):
            for way in range(2):
                n = hops(sub, way)
                if s > n:
                    continue
                far = n + 1 - s
                d = lax.rem(z + (far if way == 0 else NZ - far), NZ)
                total = grad[d // NZL, lax.rem(d, NZL), sub * 32 : (sub + 1) * 32]
                if s > 1:
                    arrived(g_copy[sub, way, s - 1])
                    total = total + g_in[sub, way, s - 2].astype(F32)
                g_out[sub, way, s - 1] = total.astype(BF16)
                step = g_in.at[sub, way, s - 1]
                offset = dict(dz=1 if way == 0 else NZ - 1)
                g_copy[sub, way, s] = remote("sum", step, (g_out.at[sub, way, s - 1], step, offset))
        if s == 1:
            arrived(o_copy)
            for y1 in range(NY_):
                for b in range(NZL):
                    e_all[:, :, b * 512 + y1 * 128 : b * 512 + (y1 + 1) * 128] = e_in[y1, :, :, b * 128 : (b + 1) * 128]
            e_done = local(e_all, (e_all, out_e))
    for x1 in range(NX_):
        total = grad[zh, zl, x1 * 32 : (x1 + 1) * 32]
        for way in range(2):
            n = hops(x1, way)
            arrived(g_copy[x1, way, n])
            total = total + g_in[x1, way, n - 1].astype(F32)
        total = total * (1.0 / 256)
        f_out[x1] = total.astype(BF16)
        f_own[x1] = total
    f_copy = remote("final", f_in.at[0:3], *[(f_out.at[lax.rem(x + d, NX_)], f_in.at[x], dict(dx=d)) for d in (1, 3, 2)])
    g_all[:, cols(x, TILE)] = f_own[x]
    arrived(f_copy)
    for d in range(1, NX_):
        x1 = lax.rem(x + d, NX_)
        g_all[:, cols(x1, TILE)] = f_in[x1].astype(F32)
    done = local(g_all, (g_all, out_g))
    e_done.wait()
    done.wait()
    sent = {
        "gain": gains.at[0], "early": t_rem.at[0], "late": t_rem.at[1], "w_x": w.at[0, 0:96], "ring": w.at[0:6],
        "far": w.at[0], "student": st_in.at[0:3], "z": z_in, "square": sq_in, "x": n_out.at[:, 0:3],
        "y": norm.at[0:2], "forward": norm.at[0], "pair": pp_in, "q": q_in.at[:, 0:3], "error": q_in.at[:, 0:3],
        "share": pp_in, "out": e_in.at[0:3], "sum": w.at[0:7], "final": f_in.at[0:3],
    }
    for kind, j in sends.items():
        pltpu.make_async_copy(sent[kind], sent[kind], send_sem.at[j]).wait()


def place(error, gradient, out_e, out_g):
    out_e[...] = error[...]
    out_g[...] = gradient[...]


def body(teacher_partial, teacher_resid, norm_gain, projector, student_hidden):
    tp = teacher_partial.reshape(2, 2, K, 16, DT)
    res = teacher_resid.reshape(2, 2, K, 16, DT)
    stu = student_hidden.reshape(2, 2, K, 16, 2048)
    hbm = pl.BlockSpec(memory_space=pl.ANY)
    vmem = pl.BlockSpec(memory_space=pltpu.VMEM)
    error, gradient = pl.pallas_call(
        kernel,
        out_shape=(jax.ShapeDtypeStruct((K, 16, 2048), BF16), jax.ShapeDtypeStruct((32, 2048), F32)),
        in_specs=[hbm] * 5,
        out_specs=(hbm, hbm),
        scratch_shapes=[
            pltpu.VMEM((2, 2, K, 16, 4096), BF16),
            pltpu.VMEM((2, 2, K, 16, 4096), BF16),
            pltpu.VMEM((2, K, 16, 4096), BF16),
            pltpu.VMEM((K, 2, 16, 4096), F32),
            pltpu.VMEM((K, 2, 16, 4096), BF16),
            pltpu.VMEM((K, 2, 16, 4096), BF16),
            pltpu.VMEM((2, 1, 2048), F32),
            pltpu.VMEM((K, 2, 16, 128), F32),
            pltpu.VMEM((K, 2, 16, 128), F32),
            pltpu.VMEM((K, 4, 2, 16, 1024), BF16),
            pltpu.VMEM((K, 4, 4, 2, 16, 1024), BF16),
            pltpu.VMEM((8, 128, 512), BF16),
            pltpu.VMEM((K, 16, 2048), BF16),
            pltpu.VMEM((4, K, 16, 512), BF16),
            pltpu.VMEM((4, K, 16, 512), BF16),
            pltpu.VMEM((2, 4, 4, 16, 512), F32),
            pltpu.VMEM((K, 4, 4, 16, 512), BF16),
            pltpu.VMEM((K, 4, 4, 16, 512), BF16),
            pltpu.VMEM((K, 4, 4, 16, 512), BF16),
            pltpu.VMEM((K, 4, 4, 16, 512), BF16),
            pltpu.VMEM((K, 4, 4, 2, 16, 512), BF16),
            pltpu.VMEM((4, K, 16, 512), BF16),
            pltpu.VMEM((2, 4, 128, 512), F32),
            pltpu.VMEM((4, 2, 4, 32, 512), BF16),
            pltpu.VMEM((4, 2, 4, 32, 512), BF16),
            pltpu.VMEM((4, 32, 512), BF16),
            pltpu.VMEM((4, 32, 512), BF16),
            pltpu.VMEM((4, 32, 512), F32),
            pltpu.VMEM((K, 16, 2048), BF16),
            pltpu.VMEM((32, 2048), F32),
            pltpu.SemaphoreType.DMA((19,)),
            pltpu.SemaphoreType.DMA((78,)),
            pltpu.SemaphoreType.DMA((16,)),
            pltpu.SemaphoreType.REGULAR((2,)),
        ],
        compiler_params=pltpu.CompilerParams(
            collective_id=0, has_side_effects=True, vmem_limit_bytes=56 << 20
        ),
        name="distill",
    )(tp, res, norm_gain.reshape(1, -1), projector, stu)
    return pl.pallas_call(
        place,
        out_shape=(jax.ShapeDtypeStruct((64, 2048), BF16), jax.ShapeDtypeStruct((32, 2048), F32)),
        in_specs=[vmem] * 2,
        out_specs=(vmem, vmem),
        name="place",
    )(error.reshape(64, 2048), gradient)


def solution(mesh):
    placed = (P("tensor", "dp", None), P("dp", None), P("tensor"), P("dp", "tensor"), P("dp", None))
    return jax.shard_map(
        body,
        mesh=mesh,
        in_specs=placed,
        out_specs=(P(("dp", "tensor"), None), P("dp", "tensor")),
        check_vma=False,
    )
```

```python
import jax
import jax.numpy as jnp
from jax import lax
from jax.experimental import pallas as pl
from jax.experimental.pallas import tpu as pltpu
from jax.sharding import PartitionSpec as P

MESH_ID = pl.DeviceIdType.MESH
F32 = jnp.float32
BF16 = jnp.bfloat16
EPS = 1e-05
DT = 8192
NX_, NY_, NZL, NZ = 4, 4, 4, 8
K = 4
TILE = 512


def dot_nt(a, b):
    return lax.dot_general(a, b, (((1,), (1,)), ((), ())), preferred_element_type=F32)


def dot_tn(a, b):
    return lax.dot_general(a, b, (((0,), (0,)), ((), ())), preferred_element_type=F32)


def kernel(
    tp, res, gain, proj, stu, out_e, out_g,
    t_own, t_rem, r_own, hid, z_out, z_in, gains, sq_out, sq_in, n_out, norm,
    w, st_raw, st_out, st_in, pp, pp_out, pp_in, q_out, q_in, err, e_in, grad, g_out, g_in, f_out, f_in, f_own,
    e_all, g_all,
    send_sem, recv_sem, local_sem, ready,
):
    dp = lax.axis_index("dp")
    tensor = lax.axis_index("tensor")
    x = lax.rem(dp, NX_)
    y = lax.rem(dp // NX_, NY_)
    zl = dp // (NX_ * NY_)
    zh = tensor // 2
    c = lax.rem(tensor, 2)
    z = zh * NZL + zl
    other = 1 - c

    def device(dx=0, dy=0, dz=0, dc=0):
        x1 = lax.rem(x + dx, NX_)
        y1 = lax.rem(y + dy, NY_)
        z1 = lax.rem(z + dz, NZ)
        c1 = lax.rem(c + dc, 2)
        return (lax.rem(z1, NZL) * (NX_ * NY_) + y1 * NX_ + x1, (z1 // NZL) * 2 + c1)

    counts = {"recv": 0, "local": 0}
    sends = {}

    def remote(kind, whole, *pairs, start=True):
        i = counts["recv"]
        counts["recv"] += 1
        j = sends.setdefault(kind, len(sends))
        copies = [
            pltpu.make_async_remote_copy(
                src, dst, send_sem.at[j], recv_sem.at[i], device_id=device(**offset), device_id_type=MESH_ID
            )
            for src, dst, offset in pairs
        ]
        if start:
            for copy in copies:
                copy.start()
        return pltpu.make_async_copy(whole, whole, recv_sem.at[i]), copies

    def local(whole, *pairs):
        i = counts["local"]
        counts["local"] += 1
        for src, dst in pairs:
            pltpu.make_async_copy(src, dst, local_sem.at[i]).start()
        return pltpu.make_async_copy(whole, whole, local_sem.at[i])

    def arrived(group):
        group[0].wait()

    def cols(index, width):
        return pl.ds(pl.multiple_of(index * width, width), width)

    half = [pl.ds(h * 2048, 2048) for h in range(2)]
    mine = [cols(2 * h + c, 2048) for h in range(2)]
    theirs = [cols(2 * h + other, 2048) for h in range(2)]
    early = [
        local(t_own.at[0, :, k], *[(tp.at[1 - zh, :, k, :, mine[h]], t_own.at[0, :, k, :, half[h]]) for h in range(2)])
        for k in range(K)
    ]
    late = [local(t_own.at[1], *[(tp.at[zh, :, :, :, mine[h]], t_own.at[1, :, :, :, half[h]]) for h in range(2)])]
    late += [local(r_own, *[(res.at[zh, :, :, :, mine[h]], r_own.at[:, :, :, half[h]]) for h in range(2)])]
    late_gain = local(gains.at[0], (gain, gains.at[zh]))
    late_student = local(st_raw, (stu.at[zh, c], st_raw))
    own_rows = w.at[z, pl.ds(pl.multiple_of(x * 32, 32), 32)]
    late_w = local(own_rows, (proj.at[:, cols(x, TILE)], own_rows))

    partners = [dict(dc=1)]
    partners += [dict(dz=d) for d in range(1, NZ)]
    partners += [dict(dx=d) for d in range(1, NX_)]
    partners += [dict(dy=d) for d in range(1, NY_)]
    barrier = pltpu.get_barrier_semaphore()
    for offset in partners:
        pl.semaphore_signal(barrier, inc=1, device_id=device(**offset), device_id_type=MESH_ID)
    pl.semaphore_wait(barrier, len(partners))

    gain_in = remote("gain", gains.at[0], (gain, gains.at[zh], dict(dz=4)))
    early_in = [
        remote(
            "early", t_rem.at[0, :, k],
            *[(tp.at[1 - zh, :, k, :, theirs[h]], t_rem.at[0, :, k, :, half[h]], dict(dc=1)) for h in range(2)],
        )
        for k in range(K)
    ]
    late_in = remote(
        "late", t_rem.at[1],
        *[(tp.at[zh, :, :, :, theirs[h]], t_rem.at[1, :, :, :, half[h]], dict(dc=1)) for h in range(2)],
    )
    w_x = remote(
        "w_x", w.at[0, 0:96],
        *[(proj.at[:, cols(lax.rem(x + d, NX_), TILE)], own_rows, dict(dx=d)) for d in range(1, NX_)],
    )

    pieces = [(k, part, h) for k in range(K) for part in range(2) for h in range(2)]
    z_copy = [
        remote(
            "z", z_in.at[k],
            *[
                (z_out.at[k, part, :, half[h]], z_in.at[k, part, :, half[h]], dict(dz=4))
                for part in range(2) for h in range(2)
            ],
            start=False,
        )
        for k in range(K)
    ]

    def send_pieces(first, last):
        for k, part, h in pieces[first:last]:
            z_copy[k][1][2 * part + h].start()

    def ring_step(s):
        right = lax.rem(z + NZ - (s - 1), NZ)
        left = lax.rem(z + (s - 1), NZ)
        return remote(
            "ring", w.at[0:2],
            (w.at[right], w.at[right], dict(dz=1)), (w.at[left], w.at[left], dict(dz=NZ - 1)),
        )

    def pair_sum(k):
        early[k].wait()
        arrived(early_in[k])

        @pl.loop(0, 4096 // TILE)
        def _(t):
            at = cols(t, TILE)
            pair = t_own[0, :, k, :, at].astype(F32) + t_rem[0, :, k, :, at].astype(F32)
            z_out[k, :, :, at] = pair.astype(BF16)

    pair_sum(0)
    send_pieces(0, 2)
    for k in range(1, K):
        pair_sum(k)
    late_w.wait()
    arrived(w_x)
    ring = ring_step(1)
    send_pieces(2, 3)

    for copy in late:
        copy.wait()
    arrived(late_in)
    for k in range(K):

        @pl.loop(0, 4096 // TILE)
        def _(t, k=k):
            at = cols(t, TILE)
            hid[k, :, :, at] = (
                r_own[:, k, :, at].astype(F32) + t_own[1, :, k, :, at].astype(F32) + t_rem[1, :, k, :, at].astype(F32)
            )

    late_student.wait()
    for y1 in range(NY_):
        for b in range(NZL):
            st_out[y1, :, :, b * 128 : (b + 1) * 128] = st_raw[:, :, b * 512 + y1 * 128 : b * 512 + (y1 + 1) * 128]
    st_own = local(st_in.at[y], (st_out.at[y], st_in.at[y]))
    st_copy = remote(
        "student", st_in.at[0:3], *[(st_out.at[lax.rem(y + d, NY_)], st_in.at[y], dict(dy=d)) for d in range(1, NY_)]
    )

    arrived(ring)
    ring = ring_step(2)
    send_pieces(3, 4)
    late_gain.wait()
    arrived(gain_in)

    x_own, x_copy, y_copy, p_copy, q_copy, e_copy, s_copy = {}, {}, {}, {}, {}, {}, {}

    def normalise(k):
        arrived(z_copy[k])

        def add(t, total):
            at = cols(t, TILE)
            value = hid[k, :, :, at] + z_in[k, :, :, at].astype(F32)
            hid[k, :, :, at] = value
            square = value * value
            for b in range(TILE // 128):
                total = total + square[:, :, b * 128 : (b + 1) * 128]
            return total

        sq_out[k] = lax.fori_loop(0, 4096 // TILE, add, jnp.zeros((2, 16, 128), F32))
        arrived(remote("square", sq_in.at[k], (sq_out.at[k], sq_in.at[k], dict(dc=1))))
        whole = jnp.sum(sq_out[k] + sq_in[k], axis=-1, keepdims=True)
        inv = lax.rsqrt(whole / DT + EPS)
        for h in range(2):

            @pl.loop(0, NX_)
            def _(x1, h=h):
                at = pl.ds(pl.multiple_of(h * 2048 + x1 * TILE, TILE), TILE)
                g = gains[h, :, cols(x1, TILE)]
                n_out[k, x1, :, :, h * TILE : (h + 1) * TILE] = (hid[k, :, :, at] * inv * g[None]).astype(BF16)

        own = norm.at[k, y, x]
        x_own[k] = local(own, (n_out.at[k, x], own))
        x_copy[k] = remote(
            "x", n_out.at[k, 0:3], *[(n_out.at[k, lax.rem(x + d, NX_)], own, dict(dx=d)) for d in range(1, NX_)]
        )

    def gather_y(k):
        x_own[k].wait()
        arrived(x_copy[k])
        block = norm.at[k, y]
        y_copy[k] = remote("y", norm.at[k, 0:2], *[(block, block, dict(dy=d)) for d in (1, NY_ - 1)])

    def forward_y(k):
        arrived(y_copy[k])
        blocks = [
            (norm.at[k, lax.rem(y + NY_ - d, NY_), 2 * i : 2 * i + 2], dict(dy=d)) for i, d in enumerate((1, NY_ - 1))
        ]
        y_copy[k] = remote("forward", norm.at[k, 0], *[(block, block, offset) for block, offset in blocks])

    def product(k, half, n):
        total = None
        for h in range(2):
            rows = norm[k, :, :, half, :, h * TILE : (h + 1) * TILE].reshape(256, TILE)
            weights = w[4 * h + 2 * n : 4 * h + 2 * n + 2].reshape(256, TILE)
            part = dot_nt(rows, weights)
            total = part if total is None else total + part
        return total.reshape(NY_, NX_, 16, 256)

    def project(k):
        arrived(y_copy[k])
        for own in (False, True):
            for n in range(2):
                total = product(k, c if own else other, n)
                if own:
                    pp[k % 2, :, :, :, n * 256 : (n + 1) * 256] = total
                else:
                    pp_out[k, :, :, :, n * 256 : (n + 1) * 256] = total.astype(BF16)
            if not own:
                p_copy[k] = remote("pair", pp_in.at[k], (pp_out.at[k], pp_in.at[k], dict(dc=1)))

    def pair_up(k):
        arrived(p_copy[k])

        @pl.loop(0, NY_)
        def _(y1):
            total = pp[k % 2, y1] + pp_in[k, y1].astype(F32)
            pp[k % 2, y1] = total
            q_out[k, y1] = total.astype(BF16)

        q_copy[k] = remote(
            "q", q_in.at[k, 0:3],
            *[(q_out.at[k, :, lax.rem(x + d, NX_)], q_in.at[k, x], dict(dx=d)) for d in range(1, NX_)],
        )

    def subtract(k):
        arrived(q_copy[k])

        @pl.loop(0, NY_)
        def _(y1):
            total = pp[k % 2, y1, x]
            for d in range(1, NX_):
                total = total + q_in[k, lax.rem(x + d, NX_), y1].astype(F32)
            err[k, y1, x, c] = (total - st_in[y1, k].astype(F32)).astype(BF16)

        own = err.at[k, :, x, c]
        e_copy[k] = remote("error", q_in.at[k, 0:3], *[(own, own, dict(dx=d)) for d in range(1, NX_)])
        e_in[y, k] = err[k, y, x, c]
        for i, d in enumerate(range(1, NY_)):
            o_copy[1][3 * k + i].start()

    def share(k):
        arrived(e_copy[k])
        rows = err.at[k, :, :, c]
        s_copy[k] = remote("share", pp_in.at[k], (rows, rows, dict(dc=1)))

    def accumulate(k):
        arrived(s_copy[k])
        e = err[k].reshape(512, 512)
        for h in range(2):
            n = norm[k, :, :, :, :, h * TILE : (h + 1) * TILE].reshape(512, TILE)
            part = dot_tn(e, n).reshape(NZL, 128, TILE)
            grad[h] = part if k == 0 else grad[h] + part

    arrived(st_copy)
    st_own.wait()
    o_copy = remote(
        "out", e_in.at[0:3],
        *[
            (err.at[k, lax.rem(y + d, NY_), x, c], e_in.at[y, k], dict(dy=d))
            for k in range(K) for d in range(1, NY_)
        ],
        start=False,
    )

    arrived(ring)
    ring = ring_step(3)
    send_pieces(4, 5)
    arrived(ring)
    right = w.at[lax.rem(z + NZ - 3, NZ), 0:64]
    left = w.at[lax.rem(z + 3, NZ), 64:128]
    ring = remote("far", w.at[0], (right, right, dict(dz=1)), (left, left, dict(dz=NZ - 1)))
    send_pieces(5, 6)
    normalise(0)
    arrived(ring)
    send_pieces(6, 8)
    pl.semaphore_signal(ready.at[0], inc=1, device_id=device(dc=1), device_id_type=MESH_ID)
    pl.semaphore_wait(ready.at[0], 1)
    for d in range(1, NZ):
        pl.semaphore_signal(ready.at[1], inc=1, device_id=device(dz=d), device_id_type=MESH_ID)
    gather_y(0)
    pl.semaphore_wait(ready.at[1], NZ - 1)
    send_pieces(8, 10)
    paced = {(normalise, 1): [(10, 12)], (gather_y, 1): [(12, 14)], (normalise, 2): [(14, 16)]}
    for stage, k in (
        (normalise, 1), (forward_y, 0), (gather_y, 1), (project, 0),
        (normalise, 2), (forward_y, 1), (gather_y, 2), (pair_up, 0), (project, 1),
        (normalise, 3), (subtract, 0), (forward_y, 2), (gather_y, 3), (pair_up, 1), (project, 2), (share, 0),
        (subtract, 1), (accumulate, 0), (pair_up, 2), (forward_y, 3), (share, 1), (project, 3), (subtract, 2),
        (pair_up, 3), (accumulate, 1), (share, 2), (subtract, 3), (accumulate, 2), (share, 3), (accumulate, 3),
    ):
        stage(k)
        for first, last in paced.get((stage, k), ()):
            send_pieces(first, last)

    def hops(sub, way):
        return 4 if sub % 2 == way else 3

    g_copy = {}
    for s in range(1, 5):
        for sub in range(4):
            for way in range(2):
                n = hops(sub, way)
                if s > n:
                    continue
                far = n + 1 - s
                d = lax.rem(z + (far if way == 0 else NZ - far), NZ)
                total = grad[d // NZL, lax.rem(d, NZL), sub * 32 : (sub + 1) * 32]
                if s > 1:
                    arrived(g_copy[sub, way, s - 1])
                    total = total + g_in[sub, way, s - 2].astype(F32)
                g_out[sub, way, s - 1] = total.astype(BF16)
                step = g_in.at[sub, way, s - 1]
                offset = dict(dz=1 if way == 0 else NZ - 1)
                g_copy[sub, way, s] = remote("sum", step, (g_out.at[sub, way, s - 1], step, offset))
        if s == 1:
            arrived(o_copy)
            for y1 in range(NY_):
                for b in range(NZL):
                    e_all[:, :, b * 512 + y1 * 128 : b * 512 + (y1 + 1) * 128] = e_in[y1, :, :, b * 128 : (b + 1) * 128]
            e_done = local(e_all, (e_all, out_e))
    for x1 in range(NX_):
        total = grad[zh, zl, x1 * 32 : (x1 + 1) * 32]
        for way in range(2):
            n = hops(x1, way)
            arrived(g_copy[x1, way, n])
            total = total + g_in[x1, way, n - 1].astype(F32)
        total = total * (1.0 / 256)
        f_out[x1] = total.astype(BF16)
        f_own[x1] = total
    f_copy = remote("final", f_in.at[0:3], *[(f_out.at[lax.rem(x + d, NX_)], f_in.at[x], dict(dx=d)) for d in (1, 3, 2)])
    g_all[:, cols(x, TILE)] = f_own[x]
    arrived(f_copy)
    for d in range(1, NX_):
        x1 = lax.rem(x + d, NX_)
        g_all[:, cols(x1, TILE)] = f_in[x1].astype(F32)
    done = local(g_all, (g_all, out_g))
    e_done.wait()
    done.wait()
    sent = {
        "gain": gains.at[0], "early": t_rem.at[0], "late": t_rem.at[1], "w_x": w.at[0, 0:96], "ring": w.at[0:6],
        "far": w.at[0], "student": st_in.at[0:3], "z": z_in, "square": sq_in, "x": n_out.at[:, 0:3],
        "y": norm.at[0:2], "forward": norm.at[0], "pair": pp_in, "q": q_in.at[:, 0:3], "error": q_in.at[:, 0:3],
        "share": pp_in, "out": e_in.at[0:3], "sum": w.at[0:7], "final": f_in.at[0:3],
    }
    for kind, j in sends.items():
        pltpu.make_async_copy(sent[kind], sent[kind], send_sem.at[j]).wait()


def place(error, gradient, out_e, out_g):
    out_e[...] = error[...]
    out_g[...] = gradient[...]


def body(teacher_partial, teacher_resid, norm_gain, projector, student_hidden):
    tp = teacher_partial.reshape(2, 2, K, 16, DT)
    res = teacher_resid.reshape(2, 2, K, 16, DT)
    stu = student_hidden.reshape(2, 2, K, 16, 2048)
    hbm = pl.BlockSpec(memory_space=pl.ANY)
    vmem = pl.BlockSpec(memory_space=pltpu.VMEM)
    error, gradient = pl.pallas_call(
        kernel,
        out_shape=(jax.ShapeDtypeStruct((K, 16, 2048), BF16), jax.ShapeDtypeStruct((32, 2048), F32)),
        in_specs=[hbm] * 5,
        out_specs=(hbm, hbm),
        scratch_shapes=[
            pltpu.VMEM((2, 2, K, 16, 4096), BF16),
            pltpu.VMEM((2, 2, K, 16, 4096), BF16),
            pltpu.VMEM((2, K, 16, 4096), BF16),
            pltpu.VMEM((K, 2, 16, 4096), F32),
            pltpu.VMEM((K, 2, 16, 4096), BF16),
            pltpu.VMEM((K, 2, 16, 4096), BF16),
            pltpu.VMEM((2, 1, 2048), F32),
            pltpu.VMEM((K, 2, 16, 128), F32),
            pltpu.VMEM((K, 2, 16, 128), F32),
            pltpu.VMEM((K, 4, 2, 16, 1024), BF16),
            pltpu.VMEM((K, 4, 4, 2, 16, 1024), BF16),
            pltpu.VMEM((8, 128, 512), BF16),
            pltpu.VMEM((K, 16, 2048), BF16),
            pltpu.VMEM((4, K, 16, 512), BF16),
            pltpu.VMEM((4, K, 16, 512), BF16),
            pltpu.VMEM((2, 4, 4, 16, 512), F32),
            pltpu.VMEM((K, 4, 4, 16, 512), BF16),
            pltpu.VMEM((K, 4, 4, 16, 512), BF16),
            pltpu.VMEM((K, 4, 4, 16, 512), BF16),
            pltpu.VMEM((K, 4, 4, 16, 512), BF16),
            pltpu.VMEM((K, 4, 4, 2, 16, 512), BF16),
            pltpu.VMEM((4, K, 16, 512), BF16),
            pltpu.VMEM((2, 4, 128, 512), F32),
            pltpu.VMEM((4, 2, 4, 32, 512), BF16),
            pltpu.VMEM((4, 2, 4, 32, 512), BF16),
            pltpu.VMEM((4, 32, 512), BF16),
            pltpu.VMEM((4, 32, 512), BF16),
            pltpu.VMEM((4, 32, 512), F32),
            pltpu.VMEM((K, 16, 2048), BF16),
            pltpu.VMEM((32, 2048), F32),
            pltpu.SemaphoreType.DMA((19,)),
            pltpu.SemaphoreType.DMA((78,)),
            pltpu.SemaphoreType.DMA((16,)),
            pltpu.SemaphoreType.REGULAR((2,)),
        ],
        compiler_params=pltpu.CompilerParams(
            collective_id=0, has_side_effects=True, vmem_limit_bytes=56 << 20
        ),
        name="distill",
    )(tp, res, norm_gain.reshape(1, -1), projector, stu)
    return pl.pallas_call(
        place,
        out_shape=(jax.ShapeDtypeStruct((64, 2048), BF16), jax.ShapeDtypeStruct((32, 2048), F32)),
        in_specs=[vmem] * 2,
        out_specs=(vmem, vmem),
        name="place",
    )(error.reshape(64, 2048), gradient)


def solution(mesh):
    placed = (P("tensor", "dp", None), P("dp", None), P("tensor"), P("dp", "tensor"), P("dp", None))
    return jax.shard_map(
        body,
        mesh=mesh,
        in_specs=placed,
        out_specs=(P(("dp", "tensor"), None), P("dp", "tensor")),
        check_vma=False,
    )
```

```python
import jax
import jax.numpy as jnp
from jax import lax
from jax.experimental import pallas as pl
from jax.experimental.pallas import tpu as pltpu
from jax.sharding import PartitionSpec as P

MESH_ID = pl.DeviceIdType.MESH
F32 = jnp.float32
BF16 = jnp.bfloat16
EPS = 1e-05
DT = 8192
NX_, NY_, NZL, NZ = 4, 4, 4, 8
K = 4
TILE = 512


def dot_nt(a, b):
    return lax.dot_general(a, b, (((1,), (1,)), ((), ())), preferred_element_type=F32)


def dot_tn(a, b):
    return lax.dot_general(a, b, (((0,), (0,)), ((), ())), preferred_element_type=F32)


def kernel(
    tp, res, gain, proj, stu, out_e, out_g,
    t_own, t_rem, r_own, hid, z_out, z_in, gains, sq_out, sq_in, n_out, norm,
    w, st_raw, st_out, st_in, pp, pp_out, pp_in, q_out, q_in, err, e_in, grad, g_out, g_in, f_out, f_in, f_own,
    e_all, g_all,
    send_sem, recv_sem, local_sem, ready,
):
    dp = lax.axis_index("dp")
    tensor = lax.axis_index("tensor")
    x = lax.rem(dp, NX_)
    y = lax.rem(dp // NX_, NY_)
    zl = dp // (NX_ * NY_)
    zh = tensor // 2
    c = lax.rem(tensor, 2)
    z = zh * NZL + zl
    other = 1 - c

    def device(dx=0, dy=0, dz=0, dc=0):
        x1 = lax.rem(x + dx, NX_)
        y1 = lax.rem(y + dy, NY_)
        z1 = lax.rem(z + dz, NZ)
        c1 = lax.rem(c + dc, 2)
        return (lax.rem(z1, NZL) * (NX_ * NY_) + y1 * NX_ + x1, (z1 // NZL) * 2 + c1)

    counts = {"recv": 0, "local": 0}
    sends = {}

    def remote(kind, whole, *pairs, start=True):
        i = counts["recv"]
        counts["recv"] += 1
        j = sends.setdefault(kind, len(sends))
        copies = [
            pltpu.make_async_remote_copy(
                src, dst, send_sem.at[j], recv_sem.at[i], device_id=device(**offset), device_id_type=MESH_ID
            )
            for src, dst, offset in pairs
        ]
        if start:
            for copy in copies:
                copy.start()
        return pltpu.make_async_copy(whole, whole, recv_sem.at[i]), copies

    def local(whole, *pairs):
        i = counts["local"]
        counts["local"] += 1
        for src, dst in pairs:
            pltpu.make_async_copy(src, dst, local_sem.at[i]).start()
        return pltpu.make_async_copy(whole, whole, local_sem.at[i])

    def arrived(group):
        group[0].wait()

    def cols(index, width):
        return pl.ds(pl.multiple_of(index * width, width), width)

    half = [pl.ds(h * 2048, 2048) for h in range(2)]
    mine = [cols(2 * h + c, 2048) for h in range(2)]
    theirs = [cols(2 * h + other, 2048) for h in range(2)]
    early = [
        local(t_own.at[0, :, k], *[(tp.at[1 - zh, :, k, :, mine[h]], t_own.at[0, :, k, :, half[h]]) for h in range(2)])
        for k in range(K)
    ]
    late = [local(t_own.at[1], *[(tp.at[zh, :, :, :, mine[h]], t_own.at[1, :, :, :, half[h]]) for h in range(2)])]
    late += [local(r_own, *[(res.at[zh, :, :, :, mine[h]], r_own.at[:, :, :, half[h]]) for h in range(2)])]
    late_gain = local(gains.at[0], (gain, gains.at[zh]))
    late_student = local(st_raw, (stu.at[zh, c], st_raw))
    own_rows = w.at[z, pl.ds(pl.multiple_of(x * 32, 32), 32)]
    late_w = local(own_rows, (proj.at[:, cols(x, TILE)], own_rows))

    partners = [dict(dc=1)]
    partners += [dict(dz=d) for d in range(1, NZ)]
    partners += [dict(dx=d) for d in range(1, NX_)]
    partners += [dict(dy=d) for d in range(1, NY_)]
    barrier = pltpu.get_barrier_semaphore()
    for offset in partners:
        pl.semaphore_signal(barrier, inc=1, device_id=device(**offset), device_id_type=MESH_ID)
    pl.semaphore_wait(barrier, len(partners))

    gain_in = remote("gain", gains.at[0], (gain, gains.at[zh], dict(dz=4)))
    w_x = remote(
        "w_x", w.at[0, 0:96],
        *[(proj.at[:, cols(lax.rem(x + d, NX_), TILE)], own_rows, dict(dx=d)) for d in range(1, NX_)],
    )
    early_in = [
        remote(
            "early", t_rem.at[0, :, k],
            *[(tp.at[1 - zh, :, k, :, theirs[h]], t_rem.at[0, :, k, :, half[h]], dict(dc=1)) for h in range(2)],
        )
        for k in range(K)
    ]
    late_in = remote(
        "late", t_rem.at[1],
        *[(tp.at[zh, :, :, :, theirs[h]], t_rem.at[1, :, :, :, half[h]], dict(dc=1)) for h in range(2)],
    )
    pieces = [(k, part, h) for k in range(K) for part in range(2) for h in range(2)]
    z_copy = [
        remote(
            "z", z_in.at[k],
            *[
                (z_out.at[k, part, :, half[h]], z_in.at[k, part, :, half[h]], dict(dz=4))
                for part in range(2) for h in range(2)
            ],
            start=False,
        )
        for k in range(K)
    ]

    def send_pieces(first, last):
        for k, part, h in pieces[first:last]:
            z_copy[k][1][2 * part + h].start()

    def ring_step(s):
        right = lax.rem(z + NZ - (s - 1), NZ)
        left = lax.rem(z + (s - 1), NZ)
        return remote(
            "ring", w.at[0:2],
            (w.at[right], w.at[right], dict(dz=1)), (w.at[left], w.at[left], dict(dz=NZ - 1)),
        )

    def pair_sum(k):
        early[k].wait()
        arrived(early_in[k])

        @pl.loop(0, 4096 // TILE)
        def _(t):
            at = cols(t, TILE)
            pair = t_own[0, :, k, :, at].astype(F32) + t_rem[0, :, k, :, at].astype(F32)
            z_out[k, :, :, at] = pair.astype(BF16)

    pair_sum(0)
    send_pieces(0, 1)
    for k in range(1, K):
        pair_sum(k)
    late_w.wait()
    arrived(w_x)
    ring = ring_step(1)
    send_pieces(1, 3)

    for copy in late:
        copy.wait()
    arrived(late_in)
    for k in range(K):

        @pl.loop(0, 4096 // TILE)
        def _(t, k=k):
            at = cols(t, TILE)
            hid[k, :, :, at] = (
                r_own[:, k, :, at].astype(F32) + t_own[1, :, k, :, at].astype(F32) + t_rem[1, :, k, :, at].astype(F32)
            )

    late_student.wait()
    for y1 in range(NY_):
        for b in range(NZL):
            st_out[y1, :, :, b * 128 : (b + 1) * 128] = st_raw[:, :, b * 512 + y1 * 128 : b * 512 + (y1 + 1) * 128]
    st_own = local(st_in.at[y], (st_out.at[y], st_in.at[y]))
    st_copy = remote(
        "student", st_in.at[0:3], *[(st_out.at[lax.rem(y + d, NY_)], st_in.at[y], dict(dy=d)) for d in range(1, NY_)]
    )

    arrived(ring)
    ring = ring_step(2)
    send_pieces(3, 4)
    late_gain.wait()
    arrived(gain_in)

    x_own, x_copy, y_copy, p_copy, q_copy, e_copy, s_copy = {}, {}, {}, {}, {}, {}, {}

    def normalise(k):
        arrived(z_copy[k])

        def add(t, total):
            at = cols(t, TILE)
            value = hid[k, :, :, at] + z_in[k, :, :, at].astype(F32)
            hid[k, :, :, at] = value
            square = value * value
            for b in range(TILE // 128):
                total = total + square[:, :, b * 128 : (b + 1) * 128]
            return total

        sq_out[k] = lax.fori_loop(0, 4096 // TILE, add, jnp.zeros((2, 16, 128), F32))
        arrived(remote("square", sq_in.at[k], (sq_out.at[k], sq_in.at[k], dict(dc=1))))
        whole = jnp.sum(sq_out[k] + sq_in[k], axis=-1, keepdims=True)
        inv = lax.rsqrt(whole / DT + EPS)
        for h in range(2):

            @pl.loop(0, NX_)
            def _(x1, h=h):
                at = pl.ds(pl.multiple_of(h * 2048 + x1 * TILE, TILE), TILE)
                g = gains[h, :, cols(x1, TILE)]
                n_out[k, x1, :, :, h * TILE : (h + 1) * TILE] = (hid[k, :, :, at] * inv * g[None]).astype(BF16)

        own = norm.at[k, y, x]
        x_own[k] = local(own, (n_out.at[k, x], own))
        x_copy[k] = remote(
            "x", n_out.at[k, 0:3], *[(n_out.at[k, lax.rem(x + d, NX_)], own, dict(dx=d)) for d in range(1, NX_)]
        )

    def gather_y(k):
        x_own[k].wait()
        arrived(x_copy[k])
        block = norm.at[k, y]
        y_copy[k] = remote("y", norm.at[k, 0:2], *[(block, block, dict(dy=d)) for d in (1, NY_ - 1)])

    def forward_y(k):
        arrived(y_copy[k])
        blocks = [
            (norm.at[k, lax.rem(y + NY_ - d, NY_), 2 * i : 2 * i + 2], dict(dy=d)) for i, d in enumerate((1, NY_ - 1))
        ]
        y_copy[k] = remote("forward", norm.at[k, 0], *[(block, block, offset) for block, offset in blocks])

    def product(k, half, n):
        total = None
        for h in range(2):
            rows = norm[k, :, :, half, :, h * TILE : (h + 1) * TILE].reshape(256, TILE)
            weights = w[4 * h + 2 * n : 4 * h + 2 * n + 2].reshape(256, TILE)
            part = dot_nt(rows, weights)
            total = part if total is None else total + part
        return total.reshape(NY_, NX_, 16, 256)

    def project(k):
        arrived(y_copy[k])
        for own in (False, True):
            for n in range(2):
                total = product(k, c if own else other, n)
                if own:
                    pp[k % 2, :, :, :, n * 256 : (n + 1) * 256] = total
                else:
                    pp_out[k, :, :, :, n * 256 : (n + 1) * 256] = total.astype(BF16)
            if not own:
                p_copy[k] = remote("pair", pp_in.at[k], (pp_out.at[k], pp_in.at[k], dict(dc=1)))

    def pair_up(k):
        arrived(p_copy[k])

        @pl.loop(0, NY_)
        def _(y1):
            total = pp[k % 2, y1] + pp_in[k, y1].astype(F32)
            pp[k % 2, y1] = total
            q_out[k, y1] = total.astype(BF16)

        q_copy[k] = remote(
            "q", q_in.at[k, 0:3],
            *[(q_out.at[k, :, lax.rem(x + d, NX_)], q_in.at[k, x], dict(dx=d)) for d in range(1, NX_)],
        )

    def subtract(k):
        arrived(q_copy[k])

        @pl.loop(0, NY_)
        def _(y1):
            total = pp[k % 2, y1, x]
            for d in range(1, NX_):
                total = total + q_in[k, lax.rem(x + d, NX_), y1].astype(F32)
            err[k, y1, x, c] = (total - st_in[y1, k].astype(F32)).astype(BF16)

        own = err.at[k, :, x, c]
        e_copy[k] = remote("error", q_in.at[k, 0:3], *[(own, own, dict(dx=d)) for d in range(1, NX_)])
        e_in[y, k] = err[k, y, x, c]
        for i, d in enumerate(range(1, NY_)):
            o_copy[1][3 * k + i].start()

    def share(k):
        arrived(e_copy[k])
        rows = err.at[k, :, :, c]
        s_copy[k] = remote("share", pp_in.at[k], (rows, rows, dict(dc=1)))

    def accumulate(k):
        arrived(s_copy[k])
        e = err[k].reshape(512, 512)
        for h in range(2):
            n = norm[k, :, :, :, :, h * TILE : (h + 1) * TILE].reshape(512, TILE)
            part = dot_tn(e, n).reshape(NZL, 128, TILE)
            grad[h] = part if k == 0 else grad[h] + part

    arrived(st_copy)
    st_own.wait()
    o_copy = remote(
        "out", e_in.at[0:3],
        *[
            (err.at[k, lax.rem(y + d, NY_), x, c], e_in.at[y, k], dict(dy=d))
            for k in range(K) for d in range(1, NY_)
        ],
        start=False,
    )

    arrived(ring)
    ring = ring_step(3)
    send_pieces(4, 5)
    arrived(ring)
    right = w.at[lax.rem(z + NZ - 3, NZ), 0:64]
    left = w.at[lax.rem(z + 3, NZ), 64:128]
    ring = remote("far", w.at[0], (right, right, dict(dz=1)), (left, left, dict(dz=NZ - 1)))
    send_pieces(5, 6)
    normalise(0)
    arrived(ring)
    send_pieces(6, 8)
    pl.semaphore_signal(ready.at[0], inc=1, device_id=device(dc=1), device_id_type=MESH_ID)
    pl.semaphore_wait(ready.at[0], 1)
    for d in range(1, NZ):
        pl.semaphore_signal(ready.at[1], inc=1, device_id=device(dz=d), device_id_type=MESH_ID)
    gather_y(0)
    pl.semaphore_wait(ready.at[1], NZ - 1)
    send_pieces(8, 10)
    paced = {(normalise, 1): [(10, 12)], (gather_y, 1): [(12, 14)], (normalise, 2): [(14, 16)]}
    for stage, k in (
        (normalise, 1), (forward_y, 0), (gather_y, 1), (project, 0),
        (normalise, 2), (forward_y, 1), (gather_y, 2), (pair_up, 0), (project, 1),
        (normalise, 3), (subtract, 0), (forward_y, 2), (gather_y, 3), (pair_up, 1), (project, 2), (share, 0),
        (subtract, 1), (accumulate, 0), (pair_up, 2), (forward_y, 3), (share, 1), (project, 3), (subtract, 2),
        (pair_up, 3), (accumulate, 1), (share, 2), (subtract, 3), (accumulate, 2), (share, 3), (accumulate, 3),
    ):
        stage(k)
        for first, last in paced.get((stage, k), ()):
            send_pieces(first, last)

    def hops(sub, way):
        return 4 if sub % 2 == way else 3

    g_copy = {}
    for s in range(1, 5):
        for sub in range(4):
            for way in range(2):
                n = hops(sub, way)
                if s > n:
                    continue
                far = n + 1 - s
                d = lax.rem(z + (far if way == 0 else NZ - far), NZ)
                total = grad[d // NZL, lax.rem(d, NZL), sub * 32 : (sub + 1) * 32]
                if s > 1:
                    arrived(g_copy[sub, way, s - 1])
                    total = total + g_in[sub, way, s - 2].astype(F32)
                g_out[sub, way, s - 1] = total.astype(BF16)
                step = g_in.at[sub, way, s - 1]
                offset = dict(dz=1 if way == 0 else NZ - 1)
                g_copy[sub, way, s] = remote("sum", step, (g_out.at[sub, way, s - 1], step, offset))
        if s == 1:
            arrived(o_copy)
            for y1 in range(NY_):
                for b in range(NZL):
                    e_all[:, :, b * 512 + y1 * 128 : b * 512 + (y1 + 1) * 128] = e_in[y1, :, :, b * 128 : (b + 1) * 128]
            e_done = local(e_all, (e_all, out_e))
    for x1 in range(NX_):
        total = grad[zh, zl, x1 * 32 : (x1 + 1) * 32]
        for way in range(2):
            n = hops(x1, way)
            arrived(g_copy[x1, way, n])
            total = total + g_in[x1, way, n - 1].astype(F32)
        total = total * (1.0 / 256)
        f_out[x1] = total.astype(BF16)
        f_own[x1] = total
    f_copy = remote("final", f_in.at[0:3], *[(f_out.at[lax.rem(x + d, NX_)], f_in.at[x], dict(dx=d)) for d in (1, 3, 2)])
    g_all[:, cols(x, TILE)] = f_own[x]
    arrived(f_copy)
    for d in range(1, NX_):
        x1 = lax.rem(x + d, NX_)
        g_all[:, cols(x1, TILE)] = f_in[x1].astype(F32)
    done = local(g_all, (g_all, out_g))
    e_done.wait()
    done.wait()
    sent = {
        "gain": gains.at[0], "early": t_rem.at[0], "late": t_rem.at[1], "w_x": w.at[0, 0:96], "ring": w.at[0:6],
        "far": w.at[0], "student": st_in.at[0:3], "z": z_in, "square": sq_in, "x": n_out.at[:, 0:3],
        "y": norm.at[0:2], "forward": norm.at[0], "pair": pp_in, "q": q_in.at[:, 0:3], "error": q_in.at[:, 0:3],
        "share": pp_in, "out": e_in.at[0:3], "sum": w.at[0:7], "final": f_in.at[0:3],
    }
    for kind, j in sends.items():
        pltpu.make_async_copy(sent[kind], sent[kind], send_sem.at[j]).wait()


def place(error, gradient, out_e, out_g):
    out_e[...] = error[...]
    out_g[...] = gradient[...]


def body(teacher_partial, teacher_resid, norm_gain, projector, student_hidden):
    tp = teacher_partial.reshape(2, 2, K, 16, DT)
    res = teacher_resid.reshape(2, 2, K, 16, DT)
    stu = student_hidden.reshape(2, 2, K, 16, 2048)
    hbm = pl.BlockSpec(memory_space=pl.ANY)
    vmem = pl.BlockSpec(memory_space=pltpu.VMEM)
    error, gradient = pl.pallas_call(
        kernel,
        out_shape=(jax.ShapeDtypeStruct((K, 16, 2048), BF16), jax.ShapeDtypeStruct((32, 2048), F32)),
        in_specs=[hbm] * 5,
        out_specs=(hbm, hbm),
        scratch_shapes=[
            pltpu.VMEM((2, 2, K, 16, 4096), BF16),
            pltpu.VMEM((2, 2, K, 16, 4096), BF16),
            pltpu.VMEM((2, K, 16, 4096), BF16),
            pltpu.VMEM((K, 2, 16, 4096), F32),
            pltpu.VMEM((K, 2, 16, 4096), BF16),
            pltpu.VMEM((K, 2, 16, 4096), BF16),
            pltpu.VMEM((2, 1, 2048), F32),
            pltpu.VMEM((K, 2, 16, 128), F32),
            pltpu.VMEM((K, 2, 16, 128), F32),
            pltpu.VMEM((K, 4, 2, 16, 1024), BF16),
            pltpu.VMEM((K, 4, 4, 2, 16, 1024), BF16),
            pltpu.VMEM((8, 128, 512), BF16),
            pltpu.VMEM((K, 16, 2048), BF16),
            pltpu.VMEM((4, K, 16, 512), BF16),
            pltpu.VMEM((4, K, 16, 512), BF16),
            pltpu.VMEM((2, 4, 4, 16, 512), F32),
            pltpu.VMEM((K, 4, 4, 16, 512), BF16),
            pltpu.VMEM((K, 4, 4, 16, 512), BF16),
            pltpu.VMEM((K, 4, 4, 16, 512), BF16),
            pltpu.VMEM((K, 4, 4, 16, 512), BF16),
            pltpu.VMEM((K, 4, 4, 2, 16, 512), BF16),
            pltpu.VMEM((4, K, 16, 512), BF16),
            pltpu.VMEM((2, 4, 128, 512), F32),
            pltpu.VMEM((4, 2, 4, 32, 512), BF16),
            pltpu.VMEM((4, 2, 4, 32, 512), BF16),
            pltpu.VMEM((4, 32, 512), BF16),
            pltpu.VMEM((4, 32, 512), BF16),
            pltpu.VMEM((4, 32, 512), F32),
            pltpu.VMEM((K, 16, 2048), BF16),
            pltpu.VMEM((32, 2048), F32),
            pltpu.SemaphoreType.DMA((19,)),
            pltpu.SemaphoreType.DMA((78,)),
            pltpu.SemaphoreType.DMA((16,)),
            pltpu.SemaphoreType.REGULAR((2,)),
        ],
        compiler_params=pltpu.CompilerParams(
            collective_id=0, has_side_effects=True, vmem_limit_bytes=56 << 20
        ),
        name="distill",
    )(tp, res, norm_gain.reshape(1, -1), projector, stu)
    return pl.pallas_call(
        place,
        out_shape=(jax.ShapeDtypeStruct((64, 2048), BF16), jax.ShapeDtypeStruct((32, 2048), F32)),
        in_specs=[vmem] * 2,
        out_specs=(vmem, vmem),
        name="place",
    )(error.reshape(64, 2048), gradient)


def solution(mesh):
    placed = (P("tensor", "dp", None), P("dp", None), P("tensor"), P("dp", "tensor"), P("dp", None))
    return jax.shard_map(
        body,
        mesh=mesh,
        in_specs=placed,
        out_specs=(P(("dp", "tensor"), None), P("dp", "tensor")),
        check_vma=False,
    )
```
